32 devices in a mesh: rep: 8 (over y, x, core), exp: 4 (over z).
Axes of the slice: x: 2, y: 2, z: 4, core: 2. Of those that a mesh axis runs over, the one named last changes fastest.
Arguments:
- tokens: bfloat16 [4096, 2048], P(('rep', 'exp')), may hold values from -6 to 6
- expert_ids: int32 [4096, 8], P(('rep', 'exp')), may hold values from 0 to 15, all different within a row; in each aligned block of 128 rows (0 to 127, 128 to 255, ...) at most 72 rows name the same one
- route_weights: float32 [4096, 8], P(('rep', 'exp')), may hold values from 0.05 to 1
- placement_map: int32 [16], replicated, may hold values from 0 to 15, each once
- w_gate: bfloat16 [16, 2048, 384], P('exp', 'rep'), may hold values from -0.125 to 0.125
- w_up: bfloat16 [16, 2048, 384], P('exp', 'rep'), may hold values from -0.125 to 0.125
- down_rows: bfloat16 [16, 2048, 384], P('exp', 'rep'), may hold values from -0.3125 to 0.3125
Outputs:
- mixed: bfloat16 [4096, 2048], P(('rep', 'exp'))
The draws below stay inside these ranges and needn't reach their ends.
Inputs may be any that keep to these rules, and one draw needn't show every extreme that they name: `expert_ids`: each row names 8 different experts. Within each device's aligned block of 128 rows no expert is named by more than 72 rows, a bound that some block reaches. `placement_map`: A permutation: every storage index is used once.
All inputs are finite; a program needn't handle non-finite values.
Results may differ from the reference program's by a relative error of at most 0.0057.
Values may be sent and summed in bfloat16 or wider, within the bound.
A program may use at most 64 MiB of HBM per device.

```python
import math
import jax
import jax.numpy as jnp
import numpy as np
from jax import lax

D = 2048
HWIN = 384
TOPK = 8
EXPERTS = 16
TOK_DEV = 128
CAP = 72
TOKENS = 4096


def block_levels(own_key, dims, split, least, high):
    factor_of = 1.0
    for dim, blocks in split:
        steps = jax.random.uniform(jax.random.fold_in(jax.random.fold_in(own_key, 6), dim), (blocks,), jnp.float32, least / len(split), high / len(split))
        factor_of = factor_of * jnp.repeat(jnp.exp(steps), dims[dim] // blocks).reshape((-1,) + (1,) * (len(dims) - 1 - dim))
    return factor_of


def assign_block(rng, own, number, rows, number_of, top, reach, skew):
    sequence = jax.random.permutation(rng, number_of)
    packed, usual = load_shares(number_of, rows * top, reach, skew, True), load_shares(number_of, rows * top, reach, skew, False)
    places = jnp.arange(number_of)

    def named(lengths, rotation):
        used = int((lengths > 0).sum())
        fixed = max(1, used // 4)
        moved = fixed + (places - fixed + rotation * (used - fixed)) % max(1, number_of - fixed)
        return jnp.zeros((number_of,), jnp.int32).at[sequence[jnp.where(places < fixed, places, moved)]].set(jnp.asarray(lengths, jnp.int32))

    lengths = jnp.where(number % 4 == 0, named(packed, number // 4), named(usual, number - number // 4 - 1))
    mixed = jax.random.permutation(jax.random.fold_in(own, 3), number_of)
    source_of, receiver = mixed[0:number_of // 2 * 2:2], mixed[1:number_of // 2 * 2:2]
    margin = jnp.minimum(lengths[source_of] - 1, reach - lengths[receiver]) // 2
    margin = jnp.where((source_of == sequence[0]) | (receiver == sequence[0]) | (lengths[receiver] == 0), 0, jnp.maximum(margin, 0))
    moved = jax.random.randint(jax.random.fold_in(own, 4), (number_of // 2,), 0, 1 << 20) % (margin + 1)
    lengths = lengths.at[source_of].add(-moved).at[receiver].add(moved)
    members = jnp.searchsorted(jnp.cumsum(lengths), jnp.arange(rows * top), side="right").astype(jnp.int32)
    grid = members.reshape(top, rows).T
    grid = grid[jax.random.permutation(jax.random.fold_in(own, 1), rows)]
    rotation = jax.random.randint(jax.random.fold_in(own, 2), (rows, 1), 0, top)
    return jnp.take_along_axis(grid, (jnp.arange(top)[None, :] + rotation) % top, axis=1)


def load_shares(number_of, total, reach, slope, full):
    loads = [(1 << 20) // math.isqrt(rank ** slope) + 1 for rank in range(1, number_of + 1)]
    largest = reach if full else min(reach, max(-(-total // number_of), total * loads[0] // sum(loads)))
    least = 1 if total - largest >= number_of - 1 else 0
    counts, rest = [largest] + [least] * (number_of - 1), total - largest - least * (number_of - 1)
    while rest > 0:
        free = [i for i in range(1, number_of) if counts[i] < largest] or [i for i in range(1, number_of) if counts[i] < reach]
        mass, budget = sum([loads[i] for i in free]), rest
        for i in free:
            addition = min(reach - counts[i], max(1, budget * loads[i] // mass), rest)
            counts[i] = counts[i] + addition
            rest = rest - addition
    return np.array(counts)


def scatter_about(own_key, shape, width, most, cuts=(), held_as=jnp.bfloat16):
    values = jax.random.normal(own_key, shape, jnp.float32) * width
    if len(cuts) > 0:
        values = block_levels(own_key, shape, cuts, -0.22, 0.18) * values
    return jnp.clip(values, min=-most, max=most).astype(held_as)


def setup_inputs(seed: int = 0) -> dict:
    seeds = jax.random.split(jax.random.key(seed), 8)
    tokens = scatter_about(seeds[0], (TOKENS, D), 1.0, 6.0, ((0, 32),))
    expert_ids_keys = jax.random.split(jax.random.fold_in(seeds[1], 1), TOKENS // TOK_DEV)
    expert_ids_turns = jax.random.permutation(jax.random.fold_in(seeds[1], 3), TOKENS // TOK_DEV)
    expert_ids = jax.vmap(lambda own, number: assign_block(jax.random.fold_in(seeds[1], 2), own, number, TOK_DEV, EXPERTS, TOPK, CAP, 1))(expert_ids_keys, expert_ids_turns).reshape((TOKENS, TOPK))
    route_weights = jnp.clip(jnp.exp(math.log(1.0) - 2.9957323 * jax.random.uniform(seeds[2], (TOKENS, TOPK), jnp.float32) ** block_levels(seeds[2], (TOKENS, TOPK), ((0, 32),), -0.2, 0.2)), 0.05, 1.0)
    placement_map = jax.random.permutation(seeds[3], EXPERTS).astype(jnp.int32)
    w_gate = scatter_about(seeds[4], (EXPERTS, D, HWIN), D ** -0.5, 0.125, ((0, 4), (1, 8)))
    w_up = scatter_about(seeds[5], (EXPERTS, D, HWIN), D ** -0.5, 0.125, ((0, 4), (1, 8)))
    down_rows = scatter_about(seeds[6], (EXPERTS, D, HWIN), HWIN ** -0.5, 0.3125, ((0, 4), (1, 8)))
    return {"tokens": tokens, "expert_ids": expert_ids, "route_weights": route_weights, "placement_map": placement_map, "w_gate": w_gate, "w_up": w_up, "down_rows": down_rows}


def reference(tokens, expert_ids, route_weights, placement_map, w_gate, w_up, down_rows):
    total_rows = tokens.shape[0]
    blocks = total_rows // TOK_DEV
    block_rows = TOK_DEV * TOPK
    slot_ids = placement_map[expert_ids].astype(jnp.int32).reshape(blocks, block_rows)
    weight_rows = route_weights.reshape(blocks, block_rows)
    row_numbers = jnp.arange(block_rows, dtype=jnp.int32)
    row_base = (jnp.arange(blocks, dtype=jnp.int32) * TOK_DEV)[:, None]

    def placed(routed):
        position = jnp.cumsum(routed) - 1
        target = jnp.where(routed == 1, position, CAP).astype(jnp.int32)
        slot_index = jnp.zeros((CAP + 1,), jnp.int32).at[target].set(row_numbers)
        live_mask = jnp.zeros((CAP + 1,), jnp.int32).at[target].set(1)
        return slot_index[:CAP], live_mask[:CAP]

    def expert_step(combined, slot_number):
        routed = (slot_ids == slot_number).astype(jnp.int32)
        slot_index, live_mask = jax.vmap(placed)(routed)
        tok_index = (row_base + slot_index // TOPK).reshape(-1).astype(jnp.int32)
        share_weight = jnp.take_along_axis(weight_rows, slot_index, axis=1) * live_mask.astype(weight_rows.dtype)
        gathered = tokens[tok_index]
        gate_value = jnp.dot(gathered, w_gate[slot_number], preferred_element_type=jnp.float32)
        up_value = jnp.dot(gathered, w_up[slot_number], preferred_element_type=jnp.float32)
        hidden = (jax.nn.silu(gate_value) * up_value).astype(jnp.bfloat16)
        result = jnp.dot(hidden, down_rows[slot_number].T, preferred_element_type=jnp.float32).astype(jnp.bfloat16)
        combined = combined.at[tok_index].add(share_weight.reshape(-1, 1) * result.astype(jnp.float32))
        return combined, None

    start = jnp.zeros((total_rows, D), jnp.float32)
    combined, unused = lax.scan(expert_step, start, jnp.arange(EXPERTS, dtype=jnp.int32))
    return combined.astype(jnp.bfloat16)
```

```python
import jax
import jax.numpy as jnp
from jax import lax
from jax.sharding import PartitionSpec as P


def on_device(tokens, expert_ids, route_weights, placement_map, w_gate, w_up, down_rows):
    experts = placement_map.shape[0]
    local_experts, _, width = w_gate.shape
    model_width = tokens.shape[1]
    expert_range = jnp.arange(experts, dtype=jnp.int32)
    slot_ids = jnp.sum(jnp.where(expert_ids[:, :, None] == expert_range, placement_map, 0), axis=2)
    share = jnp.sum(
        jnp.where(slot_ids[:, :, None] == expert_range, route_weights[:, :, None], 0.0), axis=1
    )
    rows = lax.all_gather(tokens, "exp", axis=0, tiled=True)
    share = lax.all_gather(share, "exp", axis=0, tiled=True)
    share = lax.dynamic_slice_in_dim(share, lax.axis_index("exp") * local_experts, local_experts, 1)
    gate_up = lax.all_gather(jnp.stack([w_gate, w_up]), "rep", axis=2, tiled=True)
    down = lax.all_gather(down_rows, "rep", axis=1, tiled=True)
    parts = []
    for member in range(local_experts):
        gate_value = jnp.dot(rows, gate_up[0, member], preferred_element_type=jnp.float32)
        up_value = jnp.dot(rows, gate_up[1, member], preferred_element_type=jnp.float32)
        hidden = jax.nn.silu(gate_value) * up_value * share[:, member : member + 1]
        parts.append(hidden.astype(jnp.bfloat16))
    total = 0.0
    for member in range(local_experts):
        total = total + lax.dot_general(
            parts[member], down[member], (((1,), (1,)), ((), ())), preferred_element_type=jnp.float32
        )
    mixed = lax.psum_scatter(total.astype(jnp.bfloat16), "exp", scatter_dimension=0, tiled=True)
    return mixed.astype(jnp.bfloat16)


def solution(mesh):
    return jax.shard_map(
        on_device,
        mesh=mesh,
        in_specs=(
            P(("rep", "exp"), None),
            P(("rep", "exp"), None),
            P(("rep", "exp"), None),
            P(),
            P("exp", "rep", None),
            P("exp", "rep", None),
            P("exp", "rep", None),
        ),
        out_specs=P(("rep", "exp"), None),
        check_vma=False,
    )
```

```python
import functools

import jax
import jax.numpy as jnp
from jax import lax
from jax.experimental import pallas as pl
from jax.experimental.pallas import tpu as pltpu
from jax.sharding import PartitionSpec as P

LANES = 128
MESH = pl.DeviceIdType.MESH


def flip(index, bit):
    return index + bit - 2 * bit * ((index // bit) % 2)


def flip_all(index, combo):
    bit = 1
    while bit <= combo:
        if combo & bit:
            index = flip(index, bit)
        bit *= 2
    return index


def top_stage(route, combo):
    return max(stage for stage, bit in enumerate(route) if combo & bit)


def kernel(
    reps, groups, cuts,
    tokens, ids, shares, places, w_gate, w_up, w_down,
    mixed,
    rows_buf, share_buf, gate_up, down, hidden, sums, returned,
    barrier_free_local, token_send, token_recv, share_send, share_recv,
    chunk_send, chunk_recv, back_send, back_recv,
):
    rep, grp = lax.axis_index("rep"), lax.axis_index("exp")
    local, slab, width = w_gate.shape
    tok, model = tokens.shape
    feats = slab // cuts
    total_rows = groups * tok
    chip_bits = [1 << i for i in range(1, reps.bit_length() - 1)]
    routes = [chip_bits + [1], chip_bits[::-1] + [1]]
    stages = len(chip_bits) + 1
    half, piece = slab // 2, feats // 2
    chunks = local + cuts

    def peer(distance):
        return lax.rem(grp + distance, groups)

    barrier = pltpu.get_barrier_semaphore()
    for bit in routes[0]:
        pl.semaphore_signal(barrier, inc=1, device_id=(flip(rep, bit), grp), device_id_type=MESH)
    for distance in range(1, groups):
        pl.semaphore_signal(barrier, inc=1, device_id=(rep, peer(distance)), device_id_type=MESH)

    lane = lax.broadcasted_iota(jnp.int32, (tok, LANES), 1)
    dense = jnp.zeros((tok, LANES), jnp.float32)
    for k in range(ids.shape[1]):
        dense = dense + jnp.where(lane == ids[:, k : k + 1], shares[:, k : k + 1], 0.0)
    share_buf[grp] = dense

    own_copies = [
        pltpu.make_async_copy(tokens, rows_buf.at[grp], barrier_free_local.at[0]),
        pltpu.make_async_copy(w_gate, gate_up.at[:, 0, pl.ds(rep * slab, slab)], barrier_free_local.at[1]),
        pltpu.make_async_copy(w_up, gate_up.at[:, 1, pl.ds(rep * slab, slab)], barrier_free_local.at[2]),
    ]
    for q in range(cuts):
        own_copies.append(
            pltpu.make_async_copy(
                w_down.at[:, pl.ds(q * feats, feats)],
                down.at[:, q, pl.ds(rep * feats, feats)],
                barrier_free_local.at[3 + q],
            )
        )
    pl.semaphore_wait(barrier, len(routes[0]) + groups - 1)

    def token_copy(distance):
        to = (rep, peer(distance))
        return (
            pltpu.make_async_remote_copy(
                tokens, rows_buf.at[grp], token_send.at[distance - 1], token_recv.at[distance - 1],
                device_id=to, device_id_type=MESH,
            ),
            pltpu.make_async_remote_copy(
                share_buf.at[grp], share_buf.at[grp], share_send.at[distance - 1], share_recv.at[distance - 1],
                device_id=to, device_id_type=MESH,
            ),
        )

    def spot(chunk, route, block):
        if chunk < local:
            return gate_up.at[chunk, :, pl.ds(block * slab + route * half, half)]
        return down.at[:, chunk - local, pl.ds(block * feats + route * piece, piece)]

    def parts(chunk, route, block, own):
        if chunk < local:
            at = pl.ds(block * slab + route * half, half)
            if own:
                mine = pl.ds(route * half, half)
                sources = [w_gate.at[chunk, mine], w_up.at[chunk, mine]]
            else:
                sources = [gate_up.at[chunk, 0, at], gate_up.at[chunk, 1, at]]
            return [(sources[0], gate_up.at[chunk, 0, at]), (sources[1], gate_up.at[chunk, 1, at])]
        target = spot(chunk, route, block)
        if own:
            q = chunk - local
            return [(w_down.at[:, pl.ds(q * feats + route * piece, piece)], target)]
        return [(target, target)]

    def pass_on(chunk, route, combo, first_stage):
        block = flip_all(rep, combo)
        for stage in range(first_stage, stages):
            bit = routes[route][stage]
            slot = (combo | bit) - 1
            for source, target in parts(chunk, route, block, combo == 0):
                pltpu.make_async_remote_copy(
                    source, target, chunk_send.at[chunk, route, slot], chunk_recv.at[chunk, route, slot],
                    device_id=(flip(rep, bit), grp), device_id_type=MESH,
                ).start()

    def arrival(chunk, route, combo):
        place = spot(chunk, route, flip_all(rep, combo))
        return pltpu.make_async_remote_copy(
            place, place, chunk_send.at[chunk, route, combo - 1], chunk_recv.at[chunk, route, combo - 1],
            device_id=(flip(rep, 1), grp), device_id_type=MESH,
        )

    def send_own(chunk):
        for route in range(2):
            pass_on(chunk, route, 0, 0)

    def take(chunk, stage):
        for combo in range(1, reps):
            for route in range(2):
                if top_stage(routes[route], combo) == stage:
                    arrival(chunk, route, combo).wait_recv()
                    pass_on(chunk, route, combo, stage + 1)

    block_rows = min(2 * tok, total_rows)
    span = block_rows // tok

    def wait_tokens():
        for distance in range(1, groups):
            origin = lax.rem(grp + groups - distance, groups)
            pltpu.make_async_remote_copy(
                rows_buf.at[origin], rows_buf.at[origin],
                token_send.at[distance - 1], token_recv.at[distance - 1],
                device_id=(rep, peer(distance)), device_id_type=MESH,
            ).wait_recv()
            pltpu.make_async_remote_copy(
                share_buf.at[origin], share_buf.at[origin],
                share_send.at[distance - 1], share_recv.at[distance - 1],
                device_id=(rep, peer(distance)), device_id_type=MESH,
            ).wait_recv()

    def run_gate_up(member):
        slot = grp * local + member

        @pl.loop(0, total_rows // block_rows)
        def _(i):
            at = pl.ds(i * span, span)
            x = rows_buf[at].reshape(block_rows, model)
            gate_value = jnp.dot(x, gate_up[member, 0], preferred_element_type=jnp.float32)
            up_value = jnp.dot(x, gate_up[member, 1], preferred_element_type=jnp.float32)
            dense_rows = share_buf[at].reshape(block_rows, LANES)
            weight = jnp.sum(jnp.where(places[...] == slot, dense_rows, 0.0), axis=1, keepdims=True)
            value = gate_value * up_value * weight / (1.0 + jnp.exp(-gate_value))
            hidden[member, pl.ds(i * block_rows, block_rows)] = value.astype(jnp.bfloat16)

    columns = reps * feats
    cols = min(512, columns)

    def back_copy(q, part, distance):
        at = pl.ds(part * cols, cols)
        return pltpu.make_async_remote_copy(
            sums.at[q, peer(distance), :, at],
            returned.at[q, distance - 1, :, at],
            back_send.at[q, part, distance - 1],
            back_recv.at[q, part, distance - 1],
            device_id=(rep, peer(distance)), device_id_type=MESH,
        )

    def run_down(q):
        for part in range(columns // cols):

            @pl.loop(0, total_rows // block_rows)
            def _(i):
                total = jnp.zeros((block_rows, cols), jnp.float32)
                for member in range(local):
                    total = total + lax.dot_general(
                        hidden[member, pl.ds(i * block_rows, block_rows)],
                        down[member, q, part * cols : (part + 1) * cols],
                        (((1,), (1,)), ((), ())),
                        preferred_element_type=jnp.float32,
                    )
                sums[q, pl.ds(i * span, span), :, part * cols : (part + 1) * cols] = (
                    total.astype(jnp.bfloat16).reshape(span, tok, cols)
                )

            for distance in range(1, groups):
                back_copy(q, part, distance).start()

    for distance in range(1, groups):
        for copy in token_copy(distance):
            copy.start()
    send_own(0)
    for copy in own_copies:
        copy.start()
    if chunks > 1:
        send_own(1)
    take(0, 0)
    gate_up_done = 0
    for chunk in range(chunks):
        if chunk + 2 < chunks:
            send_own(chunk + 2)
        if chunk + 1 < chunks:
            take(chunk + 1, 0)
        for stage in range(1, stages):
            take(chunk, stage)
        if chunk == 0:
            for copy in own_copies:
                copy.wait()
        ready = chunk - 1 if chunk < local else local
        if ready > 0 and gate_up_done == 0:
            wait_tokens()
        while gate_up_done < ready:
            run_gate_up(gate_up_done)
            gate_up_done += 1
        if chunk >= local:
            run_down(chunk - local)

    for q in range(cuts):
        for part in range(columns // cols):
            for distance in range(1, groups):
                back_copy(q, part, distance).wait_recv()
            value = sums[q, grp, :, part * cols : (part + 1) * cols].astype(jnp.float32)
            for distance in range(1, groups):
                value = value + returned[q, distance - 1, :, part * cols : (part + 1) * cols].astype(jnp.float32)
            value = value.astype(jnp.bfloat16)
            for j in range(cols // feats):
                start = (part * cols // feats + j) * slab + q * feats
                mixed[:, start : start + feats] = value[:, j * feats : (j + 1) * feats]

    for distance in range(1, groups):
        for copy in token_copy(distance):
            copy.wait_send()
    for chunk in range(chunks):
        for route in range(2):
            for combo in range(1, reps):
                arrival(chunk, route, combo).wait_send()
    for q in range(cuts):
        for part in range(columns // cols):
            for distance in range(1, groups):
                back_copy(q, part, distance).wait_send()


def on_device(tokens, expert_ids, route_weights, placement_map, w_gate, w_up, down_rows):
    reps, groups = lax.axis_size("rep"), lax.axis_size("exp")
    local, slab, width = w_gate.shape
    tok, model = tokens.shape
    cuts = max(1, slab // LANES)
    feats = slab // cuts
    columns = reps * feats
    parts = columns // min(512, columns)
    chunks = local + cuts
    places = jnp.pad(placement_map, (0, LANES - placement_map.shape[0]), constant_values=-1).reshape(1, LANES)
    vmem, anywhere = pl.BlockSpec(memory_space=pltpu.VMEM), pl.BlockSpec(memory_space=pl.ANY)
    dma = pltpu.SemaphoreType.DMA
    return pl.pallas_call(
        functools.partial(kernel, reps, groups, cuts),
        out_shape=jax.ShapeDtypeStruct((tok, model), jnp.bfloat16),
        in_specs=[vmem, vmem, vmem, vmem, anywhere, anywhere, anywhere],
        out_specs=vmem,
        scratch_shapes=[
            pltpu.VMEM((groups, tok, model), jnp.bfloat16),
            pltpu.VMEM((groups, tok, LANES), jnp.float32),
            pltpu.VMEM((local, 2, reps * slab, width), jnp.bfloat16),
            pltpu.VMEM((local, cuts, columns, width), jnp.bfloat16),
            pltpu.VMEM((local, groups * tok, width), jnp.bfloat16),
            pltpu.VMEM((cuts, groups, tok, columns), jnp.bfloat16),
            pltpu.VMEM((cuts, groups - 1, tok, columns), jnp.bfloat16),
            dma((3 + cuts,)),
            dma((groups - 1,)),
            dma((groups - 1,)),
            dma((groups - 1,)),
            dma((groups - 1,)),
            dma((chunks, 2, reps - 1)),
            dma((chunks, 2, reps - 1)),
            dma((cuts, parts, groups - 1)),
            dma((cuts, parts, groups - 1)),
        ],
        compiler_params=pltpu.CompilerParams(
            collective_id=0, has_side_effects=True, vmem_limit_bytes=56 * 2**20
        ),
        cost_estimate=pl.CostEstimate(
            flops=6 * groups * tok * local * model * width,
            bytes_accessed=6 * local * slab * width + 4 * tok * model,
            transcendentals=groups * tok * local * width,
        ),
    )(tokens, expert_ids, route_weights, places, w_gate, w_up, down_rows)


def solution(mesh):
    return jax.shard_map(
        on_device,
        mesh=mesh,
        in_specs=(
            P(("rep", "exp"), None),
            P(("rep", "exp"), None),
            P(("rep", "exp"), None),
            P(),
            P("exp", "rep", None),
            P("exp", "rep", None),
            P("exp", "rep", None),
        ),
        out_specs=P(("rep", "exp"), None),
        check_vma=False,
    )
```

```python
import functools

import jax
import jax.numpy as jnp
from jax import lax
from jax.experimental import pallas as pl
from jax.experimental.pallas import tpu as pltpu
from jax.sharding import PartitionSpec as P

LANES = 128
MESH = pl.DeviceIdType.MESH


def flip(index, bit):
    return index + bit - 2 * bit * ((index // bit) % 2)


def flip_all(index, combo):
    bit = 1
    while bit <= combo:
        if combo & bit:
            index = flip(index, bit)
        bit *= 2
    return index


def top_stage(route, combo):
    return max(stage for stage, bit in enumerate(route) if combo & bit)


def kernel(
    reps, groups, cuts,
    tokens, ids, shares, placement, w_gate, w_up, w_down,
    mixed,
    rows_buf, share_buf, gate_up, down, hidden, sums, returned,
    local_sem, token_send, token_recv, share_send, share_recv,
    chunk_send, chunk_recv, back_send, back_recv,
):
    rep, grp = lax.axis_index("rep"), lax.axis_index("exp")
    local, slab, width = w_gate.shape
    tok, model = tokens.shape
    feats = slab // cuts
    total_rows = groups * tok
    chip_bits = [1 << i for i in range(1, reps.bit_length() - 1)]
    routes = [chip_bits + [1], chip_bits[::-1] + [1]]
    stages = len(chip_bits) + 1
    half, piece = slab // 2, feats // 2
    chunks = local + cuts

    masks = [(2 << i) - 1 for i in range(groups.bit_length() - 1)]
    paths = {0: ()}
    for mask in masks:
        paths.update({at ^ mask: path + (mask,) for at, path in list(paths.items())})

    barrier = pltpu.get_barrier_semaphore()
    for bit in routes[0]:
        pl.semaphore_signal(barrier, inc=1, device_id=(flip(rep, bit), grp), device_id_type=MESH)
    for mask in masks:
        pl.semaphore_signal(barrier, inc=1, device_id=(rep, flip_all(grp, mask)), device_id_type=MESH)

    row = lax.broadcasted_iota(jnp.int32, (LANES, tok), 0)
    dense = jnp.zeros((LANES, tok), jnp.float32)
    for k in range(ids.shape[0]):
        dense = dense + jnp.where(row == ids[k : k + 1, :], shares[k : k + 1, :], 0.0)
    lane = lax.broadcasted_iota(jnp.int32, (1, LANES), 1)
    places = jnp.full((1, LANES), -1, jnp.int32)
    for expert in range(placement.shape[0]):
        places = jnp.where(lane == expert, placement[expert], places)
    share_buf[grp] = dense.T

    own_copies = [
        pltpu.make_async_copy(tokens, rows_buf.at[grp], local_sem.at[0]),
        pltpu.make_async_copy(w_gate, gate_up.at[:, 0, pl.ds(rep * slab, slab)], local_sem.at[1]),
        pltpu.make_async_copy(w_up, gate_up.at[:, 1, pl.ds(rep * slab, slab)], local_sem.at[2]),
    ]
    for q in range(cuts):
        own_copies.append(
            pltpu.make_async_copy(
                w_down.at[:, pl.ds(q * feats, feats)],
                down.at[:, q, pl.ds(rep * feats, feats)],
                local_sem.at[3 + q],
            )
        )
    pl.semaphore_wait(barrier, len(routes[0]) + len(masks))

    def token_copies(offset, mask):
        block, slot, to = flip_all(grp, offset), (offset ^ mask) - 1, (rep, flip_all(grp, mask))
        source = tokens if offset == 0 else rows_buf.at[block]
        return (
            pltpu.make_async_remote_copy(
                source, rows_buf.at[block], token_send.at[slot], token_recv.at[slot],
                device_id=to, device_id_type=MESH,
            ),
            pltpu.make_async_remote_copy(
                share_buf.at[block], share_buf.at[block], share_send.at[slot], share_recv.at[slot],
                device_id=to, device_id_type=MESH,
            ),
        )

    def token_arrivals(offset):
        block, slot, to = flip_all(grp, offset), offset - 1, (rep, flip_all(grp, 1))
        return (
            pltpu.make_async_remote_copy(
                rows_buf.at[block], rows_buf.at[block], token_send.at[slot], token_recv.at[slot],
                device_id=to, device_id_type=MESH,
            ),
            pltpu.make_async_remote_copy(
                share_buf.at[block], share_buf.at[block], share_send.at[slot], share_recv.at[slot],
                device_id=to, device_id_type=MESH,
            ),
        )

    def send_tokens(offset):
        least = min(paths[offset], default=groups)
        for mask in masks[::-1]:
            if mask < least:
                for copy in token_copies(offset, mask):
                    copy.start()

    def take_tokens(last):
        for offset in sorted(range(1, groups), key=lambda at: len(paths[at])):
            if (min(paths[offset]) == 1) == last:
                for copy in token_arrivals(offset):
                    copy.wait_recv()
                send_tokens(offset)

    def spot(chunk, route, block):
        if chunk < local:
            return gate_up.at[chunk, :, pl.ds(block * slab + route * half, half)]
        return down.at[:, chunk - local, pl.ds(block * feats + route * piece, piece)]

    def parts(chunk, route, block, own):
        if chunk < local:
            at = pl.ds(block * slab + route * half, half)
            if own:
                mine = pl.ds(route * half, half)
                sources = [w_gate.at[chunk, mine], w_up.at[chunk, mine]]
            else:
                sources = [gate_up.at[chunk, 0, at], gate_up.at[chunk, 1, at]]
            return [(sources[0], gate_up.at[chunk, 0, at]), (sources[1], gate_up.at[chunk, 1, at])]
        target = spot(chunk, route, block)
        if own:
            q = chunk - local
            return [(w_down.at[:, pl.ds(q * feats + route * piece, piece)], target)]
        return [(target, target)]

    def pass_on(chunk, route, combo, first_stage):
        block = flip_all(rep, combo)
        for stage in range(first_stage, stages):
            bit = routes[route][stage]
            slot = (combo | bit) - 1
            for source, target in parts(chunk, route, block, combo == 0):
                pltpu.make_async_remote_copy(
                    source, target, chunk_send.at[chunk, route, slot], chunk_recv.at[chunk, route, slot],
                    device_id=(flip(rep, bit), grp), device_id_type=MESH,
                ).start()

    def arrival(chunk, route, combo):
        place = spot(chunk, route, flip_all(rep, combo))
        return pltpu.make_async_remote_copy(
            place, place, chunk_send.at[chunk, route, combo - 1], chunk_recv.at[chunk, route, combo - 1],
            device_id=(flip(rep, 1), grp), device_id_type=MESH,
        )

    def send_own(chunk):
        for route in range(2):
            pass_on(chunk, route, 0, 0)

    def take(chunk, stage):
        for combo in range(1, reps):
            for route in range(2):
                if top_stage(routes[route], combo) == stage:
                    arrival(chunk, route, combo).wait_recv()
                    pass_on(chunk, route, combo, stage + 1)

    block_rows = min(2 * tok, total_rows)
    span = block_rows // tok

    def run_gate_up(member):
        @pl.loop(0, total_rows // block_rows)
        def _(i):
            at = pl.ds(i * span, span)
            x = rows_buf[at].reshape(block_rows, model)
            gate_value = jnp.dot(x, gate_up[member, 0], preferred_element_type=jnp.float32)
            up_value = jnp.dot(x, gate_up[member, 1], preferred_element_type=jnp.float32)
            value = gate_value * up_value / (1.0 + jnp.exp(-gate_value))
            hidden[member, pl.ds(i * block_rows, block_rows)] = value.astype(jnp.bfloat16)

    columns = reps * feats
    cols = min(512, columns)

    def back_copy(q, part, offset, mask):
        at = pl.ds(part * cols, cols)
        block = flip_all(grp, offset)
        slot = offset - 1
        return pltpu.make_async_remote_copy(
            sums.at[q, block, :, at],
            returned.at[q, slot, :, at],
            back_send.at[q, part, slot],
            back_recv.at[q, part, slot],
            device_id=(rep, flip_all(grp, mask)), device_id_type=MESH,
        )

    def with_first(mask):
        return sorted((at for at in paths if at and paths[at][0] == mask), key=lambda at: -len(paths[at]))

    def run_down(q, part):
        @pl.loop(0, total_rows // block_rows)
        def _(i):
            at = pl.ds(i * span, span)
            dense_rows = share_buf[at].reshape(block_rows, LANES)
            total = jnp.zeros((block_rows, cols), jnp.float32)
            for member in range(local):
                weight = jnp.sum(
                    jnp.where(places == grp * local + member, dense_rows, 0.0), axis=1, keepdims=True
                )
                total = total + weight * lax.dot_general(
                    hidden[member, pl.ds(i * block_rows, block_rows)],
                    down[member, q, part * cols : (part + 1) * cols],
                    (((1,), (1,)), ((), ())),
                    preferred_element_type=jnp.float32,
                )
            sums[q, at, :, part * cols : (part + 1) * cols] = total.astype(jnp.bfloat16).reshape(span, tok, cols)

        send_back(q, part, 0)

    def send_back(q, part, level):
        for offset in with_first(masks[level]):
            back_copy(q, part, offset, masks[level]).start()

    def merge_back(q, part, level):
        for offset in with_first(masks[level]):
            back_copy(q, part, offset, masks[level]).wait_recv()
        for offset in with_first(masks[level]):
            rest = offset ^ masks[level]
            if rest:
                back_copy(q, part, offset, masks[level]).wait_send()
                block = flip_all(grp, rest)
                at = slice(part * cols, (part + 1) * cols)
                sums[q, block, :, at] = (
                    sums[q, block, :, at].astype(jnp.float32) + returned[q, offset - 1, :, at].astype(jnp.float32)
                ).astype(jnp.bfloat16)
        if level + 1 < len(masks):
            send_back(q, part, level + 1)

    send_tokens(0)
    send_own(0)
    for copy in own_copies:
        copy.start()
    send_own(1)
    take(0, 0)
    pieces = [(q, part) for q in range(cuts) for part in range(columns // cols)]
    gate_up_done, merged, own_sent = 0, 0, 2
    for chunk in range(chunks):
        while own_sent < min(chunk + (3 if chunk + 2 < local else 4), chunks):
            send_own(own_sent)
            own_sent += 1
        if chunk + 1 < chunks:
            take(chunk + 1, 0)
        for stage in range(1, stages):
            take(chunk, stage)
        if chunk == 0:
            for copy in own_copies:
                copy.wait()
            take_tokens(False)
        if chunk == min(local - 1, 2):
            take_tokens(True)
        if chunk >= min(local - 1, 2):
            while gate_up_done < min(chunk + 1, local):
                run_gate_up(gate_up_done)
                gate_up_done += 1
        if chunk >= local:
            for part in range(columns // cols):
                run_down(chunk - local, part)
                now = pieces.index((chunk - local, part))
                if now - merged >= 1:
                    merge_back(*pieces[merged], 0)
                    merged += 1
    while merged < len(pieces):
        merge_back(*pieces[merged], 0)
        merged += 1
    for level in range(1, len(masks)):
        for piece_at in pieces:
            merge_back(*piece_at, level)

    for q, part in pieces:
        at = slice(part * cols, (part + 1) * cols)
        value = sums[q, grp, :, at].astype(jnp.float32)
        for mask in masks:
            value = value + returned[q, mask - 1, :, at].astype(jnp.float32)
        value = value.astype(jnp.bfloat16)
        for j in range(cols // feats):
            start = (part * cols // feats + j) * slab + q * feats
            mixed[:, start : start + feats] = value[:, j * feats : (j + 1) * feats]

    for offset in range(1, groups):
        for copy in token_arrivals(offset):
            copy.wait_send()
    for chunk in range(chunks):
        for route in range(2):
            for combo in range(1, reps):
                arrival(chunk, route, combo).wait_send()
    for q, part in pieces:
        for level, mask in enumerate(masks):
            for offset in with_first(mask):
                if offset == mask:
                    back_copy(q, part, offset, mask).wait_send()


def on_device(tokens, expert_ids, route_weights, placement_map, w_gate, w_up, down_rows):
    reps, groups = lax.axis_size("rep"), lax.axis_size("exp")
    local, slab, width = w_gate.shape
    tok, model = tokens.shape
    cuts = max(1, slab // 64)
    feats = slab // cuts
    columns = reps * feats
    parts = columns // min(512, columns)
    chunks = local + cuts
    vmem, anywhere = pl.BlockSpec(memory_space=pltpu.VMEM), pl.BlockSpec(memory_space=pl.ANY)
    dma = pltpu.SemaphoreType.DMA
    return pl.pallas_call(
        functools.partial(kernel, reps, groups, cuts),
        out_shape=jax.ShapeDtypeStruct((tok, model), jnp.bfloat16),
        in_specs=[vmem, vmem, vmem, pl.BlockSpec(memory_space=pltpu.SMEM), anywhere, anywhere, anywhere],
        out_specs=vmem,
        scratch_shapes=[
            pltpu.VMEM((groups, tok, model), jnp.bfloat16),
            pltpu.VMEM((groups, tok, LANES), jnp.float32),
            pltpu.VMEM((local, 2, reps * slab, width), jnp.bfloat16),
            pltpu.VMEM((local, cuts, columns, width), jnp.bfloat16),
            pltpu.VMEM((local, groups * tok, width), jnp.bfloat16),
            pltpu.VMEM((cuts, groups, tok, columns), jnp.bfloat16),
            pltpu.VMEM((cuts, groups - 1, tok, columns), jnp.bfloat16),
            dma((3 + cuts,)),
            dma((groups - 1,)),
            dma((groups - 1,)),
            dma((groups - 1,)),
            dma((groups - 1,)),
            dma((chunks, 2, reps - 1)),
            dma((chunks, 2, reps - 1)),
            dma((cuts, parts, groups - 1)),
            dma((cuts, parts, groups - 1)),
        ],
        compiler_params=pltpu.CompilerParams(
            collective_id=0, has_side_effects=True, vmem_limit_bytes=56 * 2**20
        ),
        cost_estimate=pl.CostEstimate(
            flops=6 * groups * tok * local * model * width,
            bytes_accessed=6 * local * slab * width + 4 * tok * model,
            transcendentals=groups * tok * local * width,
        ),
    )(tokens, expert_ids.T, route_weights.T, placement_map, w_gate, w_up, down_rows)


def solution(mesh):
    return jax.shard_map(
        on_device,
        mesh=mesh,
        in_specs=(
            P(("rep", "exp"), None),
            P(("rep", "exp"), None),
            P(("rep", "exp"), None),
            P(),
            P("exp", "rep", None),
            P("exp", "rep", None),
            P("exp", "rep", None),
        ),
        out_specs=P(("rep", "exp"), None),
        check_vma=False,
    )
```

```python
import functools

import jax
import jax.numpy as jnp
from jax import lax
from jax.experimental import pallas as pl
from jax.experimental.pallas import tpu as pltpu
from jax.sharding import PartitionSpec as P

LANES = 128
MESH = pl.DeviceIdType.MESH


def flip(index, bit):
    return index + bit - 2 * bit * ((index // bit) % 2)


def flip_all(index, combo):
    bit = 1
    while bit <= combo:
        if combo & bit:
            index = flip(index, bit)
        bit *= 2
    return index


def top_stage(route, combo):
    return max(stage for stage, bit in enumerate(route) if combo & bit)


def kernel(
    reps, groups, cuts,
    tokens, ids, shares, placement, w_gate, w_up, w_down,
    mixed,
    rows_buf, share_buf, gate_up, down, hidden, sums, returned,
    local_sem, token_send, token_recv, share_send, share_recv,
    chunk_send, chunk_recv, back_send, back_recv,
):
    rep, grp = lax.axis_index("rep"), lax.axis_index("exp")
    local, slab, width = w_gate.shape
    tok, model = tokens.shape
    feats = slab // cuts
    total_rows = groups * tok
    chip_bits = [1 << i for i in range(1, reps.bit_length() - 1)]
    routes = [chip_bits + [1], chip_bits[::-1] + [1]]
    stages = len(chip_bits) + 1
    half, piece = slab // 2, feats // 2
    chunks = local + cuts

    masks = [(2 << i) - 1 for i in range(groups.bit_length() - 1)]
    paths = {0: ()}
    for mask in masks:
        paths.update({at ^ mask: path + (mask,) for at, path in list(paths.items())})

    barrier = pltpu.get_barrier_semaphore()
    for bit in routes[0]:
        pl.semaphore_signal(barrier, inc=1, device_id=(flip(rep, bit), grp), device_id_type=MESH)
    for mask in masks:
        pl.semaphore_signal(barrier, inc=1, device_id=(rep, flip_all(grp, mask)), device_id_type=MESH)

    row = lax.broadcasted_iota(jnp.int32, (LANES, tok), 0)
    dense = jnp.zeros((LANES, tok), jnp.float32)
    for k in range(ids.shape[0]):
        dense = dense + jnp.where(row == ids[k : k + 1, :], shares[k : k + 1, :], 0.0)
    lane = lax.broadcasted_iota(jnp.int32, (1, LANES), 1)
    places = jnp.full((1, LANES), -1, jnp.int32)
    for expert in range(placement.shape[0]):
        places = jnp.where(lane == expert, placement[expert], places)
    share_buf[grp] = dense.T

    own_copies = [
        pltpu.make_async_copy(tokens, rows_buf.at[grp], local_sem.at[0]),
        pltpu.make_async_copy(w_gate, gate_up.at[:, 0, pl.ds(rep * slab, slab)], local_sem.at[1]),
        pltpu.make_async_copy(w_up, gate_up.at[:, 1, pl.ds(rep * slab, slab)], local_sem.at[2]),
    ]
    for q in range(cuts):
        own_copies.append(
            pltpu.make_async_copy(
                w_down.at[:, pl.ds(q * feats, feats)],
                down.at[:, q, pl.ds(rep * feats, feats)],
                local_sem.at[3 + q],
            )
        )
    pl.semaphore_wait(barrier, len(routes[0]) + len(masks))

    def token_copies(offset, mask):
        block, slot, to = flip_all(grp, offset), (offset ^ mask) - 1, (rep, flip_all(grp, mask))
        source = tokens if offset == 0 else rows_buf.at[block]
        return (
            pltpu.make_async_remote_copy(
                source, rows_buf.at[block], token_send.at[slot], token_recv.at[slot],
                device_id=to, device_id_type=MESH,
            ),
            pltpu.make_async_remote_copy(
                share_buf.at[block], share_buf.at[block], share_send.at[slot], share_recv.at[slot],
                device_id=to, device_id_type=MESH,
            ),
        )

    def token_arrivals(offset):
        block, slot, to = flip_all(grp, offset), offset - 1, (rep, flip_all(grp, 1))
        return (
            pltpu.make_async_remote_copy(
                rows_buf.at[block], rows_buf.at[block], token_send.at[slot], token_recv.at[slot],
                device_id=to, device_id_type=MESH,
            ),
            pltpu.make_async_remote_copy(
                share_buf.at[block], share_buf.at[block], share_send.at[slot], share_recv.at[slot],
                device_id=to, device_id_type=MESH,
            ),
        )

    def send_tokens(offset):
        least = min(paths[offset], default=groups)
        for mask in masks[::-1]:
            if mask < least:
                for copy in token_copies(offset, mask):
                    copy.start()

    def take_tokens(last):
        for offset in sorted(range(1, groups), key=lambda at: len(paths[at])):
            if (min(paths[offset]) == 1) == last:
                for copy in token_arrivals(offset):
                    copy.wait_recv()
                send_tokens(offset)

    def spot(chunk, route, block):
        if chunk < local:
            return gate_up.at[chunk, :, pl.ds(block * slab + route * half, half)]
        return down.at[:, chunk - local, pl.ds(block * feats + route * piece, piece)]

    def parts(chunk, route, block, own):
        if chunk < local:
            at = pl.ds(block * slab + route * half, half)
            if own:
                mine = pl.ds(route * half, half)
                sources = [w_gate.at[chunk, mine], w_up.at[chunk, mine]]
            else:
                sources = [gate_up.at[chunk, 0, at], gate_up.at[chunk, 1, at]]
            return [(sources[0], gate_up.at[chunk, 0, at]), (sources[1], gate_up.at[chunk, 1, at])]
        target = spot(chunk, route, block)
        if own:
            q = chunk - local
            return [(w_down.at[:, pl.ds(q * feats + route * piece, piece)], target)]
        return [(target, target)]

    def pass_on(chunk, route, combo, first_stage):
        block = flip_all(rep, combo)
        for stage in range(first_stage, stages):
            bit = routes[route][stage]
            slot = (combo | bit) - 1
            for source, target in parts(chunk, route, block, combo == 0):
                pltpu.make_async_remote_copy(
                    source, target, chunk_send.at[chunk, route, slot], chunk_recv.at[chunk, route, slot],
                    device_id=(flip(rep, bit), grp), device_id_type=MESH,
                ).start()

    def arrival(chunk, route, combo):
        place = spot(chunk, route, flip_all(rep, combo))
        return pltpu.make_async_remote_copy(
            place, place, chunk_send.at[chunk, route, combo - 1], chunk_recv.at[chunk, route, combo - 1],
            device_id=(flip(rep, 1), grp), device_id_type=MESH,
        )

    def send_own(chunk):
        for route in range(2):
            pass_on(chunk, route, 0, 0)

    def take(chunk, stage):
        for combo in range(1, reps):
            for route in range(2):
                if top_stage(routes[route], combo) == stage:
                    arrival(chunk, route, combo).wait_recv()
                    pass_on(chunk, route, combo, stage + 1)

    block_rows = min(2 * tok, total_rows)
    span = block_rows // tok

    def run_gate_up(member):
        @pl.loop(0, total_rows // block_rows)
        def _(i):
            at = pl.ds(i * span, span)
            x = rows_buf[at].reshape(block_rows, model)
            gate_value = jnp.dot(x, gate_up[member, 0], preferred_element_type=jnp.float32)
            up_value = jnp.dot(x, gate_up[member, 1], preferred_element_type=jnp.float32)
            value = gate_value * up_value / (1.0 + jnp.exp(-gate_value))
            hidden[member, pl.ds(i * block_rows, block_rows)] = value.astype(jnp.bfloat16)

    columns = reps * feats
    cols = min(256, columns)

    def back_copy(q, part, offset, mask):
        at = pl.ds(part * cols, cols)
        block = flip_all(grp, offset)
        slot = offset - 1
        return pltpu.make_async_remote_copy(
            sums.at[q, block, :, at],
            returned.at[q, slot, :, at],
            back_send.at[q, part, slot],
            back_recv.at[q, part, slot],
            device_id=(rep, flip_all(grp, mask)), device_id_type=MESH,
        )

    def with_first(mask):
        return sorted((at for at in paths if at and paths[at][0] == mask), key=lambda at: -len(paths[at]))

    def run_down(q, part):
        @pl.loop(0, total_rows // block_rows)
        def _(i):
            at = pl.ds(i * span, span)
            dense_rows = share_buf[at].reshape(block_rows, LANES)
            total = jnp.zeros((block_rows, cols), jnp.float32)
            for member in range(local):
                weight = jnp.sum(
                    jnp.where(places == grp * local + member, dense_rows, 0.0), axis=1, keepdims=True
                )
                total = total + weight * lax.dot_general(
                    hidden[member, pl.ds(i * block_rows, block_rows)],
                    down[member, q, part * cols : (part + 1) * cols],
                    (((1,), (1,)), ((), ())),
                    preferred_element_type=jnp.float32,
                )
            sums[q, at, :, part * cols : (part + 1) * cols] = total.astype(jnp.bfloat16).reshape(span, tok, cols)

        send_back(q, part, 0)

    def send_back(q, part, level):
        for offset in with_first(masks[level]):
            back_copy(q, part, offset, masks[level]).start()

    def merge_back(q, part, level):
        for offset in with_first(masks[level]):
            back_copy(q, part, offset, masks[level]).wait_recv()
        for offset in with_first(masks[level]):
            rest = offset ^ masks[level]
            if rest:
                back_copy(q, part, offset, masks[level]).wait_send()
                block = flip_all(grp, rest)
                at = slice(part * cols, (part + 1) * cols)
                sums[q, block, :, at] = (
                    sums[q, block, :, at].astype(jnp.float32) + returned[q, offset - 1, :, at].astype(jnp.float32)
                ).astype(jnp.bfloat16)
        if level + 1 < len(masks):
            send_back(q, part, level + 1)

    send_tokens(0)
    send_own(0)
    for copy in own_copies:
        copy.start()
    send_own(1)
    take(0, 0)
    pieces = [(q, part) for q in range(cuts) for part in range(columns // cols)]
    gate_up_done, merged, own_sent = 0, 0, 2
    for chunk in range(chunks):
        while own_sent < min(chunk + (3 if chunk + 2 < local else 4), chunks):
            send_own(own_sent)
            own_sent += 1
        if chunk + 1 < chunks:
            take(chunk + 1, 0)
        first = min(local - 1, 2)
        if chunk == first:
            if chunk == 0:
                take_tokens(False)
            take_tokens(True)
        for stage in range(1, stages):
            if chunk == first and gate_up_done < chunk:
                run_gate_up(gate_up_done)
                gate_up_done += 1
            take(chunk, stage)
        if chunk == 0:
            for copy in own_copies:
                copy.wait()
            if first > 0:
                take_tokens(False)
        if chunk >= first:
            while gate_up_done < min(chunk + 1, local):
                run_gate_up(gate_up_done)
                gate_up_done += 1
        if chunk >= local:
            for part in range(columns // cols):
                run_down(chunk - local, part)
                now = pieces.index((chunk - local, part))
                if now - merged >= 2:
                    merge_back(*pieces[merged], 0)
                    merged += 1
    for offset in range(1, groups):
        for copy in token_arrivals(offset):
            copy.wait_send()
    for chunk in range(chunks):
        for route in range(2):
            for combo in range(1, reps):
                arrival(chunk, route, combo).wait_send()
    while merged < len(pieces):
        merge_back(*pieces[merged], 0)
        merged += 1
    for level in range(1, len(masks) - 1):
        for piece_at in pieces:
            merge_back(*piece_at, level)

    for q, part in pieces:
        merge_back(q, part, len(masks) - 1)
        at = slice(part * cols, (part + 1) * cols)
        value = sums[q, grp, :, at].astype(jnp.float32)
        for mask in masks:
            value = value + returned[q, mask - 1, :, at].astype(jnp.float32)
        value = value.astype(jnp.bfloat16)
        for j in range(cols // feats):
            start = (part * cols // feats + j) * slab + q * feats
            mixed[:, start : start + feats] = value[:, j * feats : (j + 1) * feats]

    for q, part in pieces:
        for level, mask in enumerate(masks):
            for offset in with_first(mask):
                if offset == mask:
                    back_copy(q, part, offset, mask).wait_send()


def on_device(tokens, expert_ids, route_weights, placement_map, w_gate, w_up, down_rows):
    reps, groups = lax.axis_size("rep"), lax.axis_size("exp")
    local, slab, width = w_gate.shape
    tok, model = tokens.shape
    cuts = max(1, slab // 64)
    feats = slab // cuts
    columns = reps * feats
    parts = columns // min(256, columns)
    chunks = local + cuts
    vmem, anywhere = pl.BlockSpec(memory_space=pltpu.VMEM), pl.BlockSpec(memory_space=pl.ANY)
    dma = pltpu.SemaphoreType.DMA
    return pl.pallas_call(
        functools.partial(kernel, reps, groups, cuts),
        out_shape=jax.ShapeDtypeStruct((tok, model), jnp.bfloat16),
        in_specs=[vmem, vmem, vmem, pl.BlockSpec(memory_space=pltpu.SMEM), anywhere, anywhere, anywhere],
        out_specs=vmem,
        scratch_shapes=[
            pltpu.VMEM((groups, tok, model), jnp.bfloat16),
            pltpu.VMEM((groups, tok, LANES), jnp.float32),
            pltpu.VMEM((local, 2, reps * slab, width), jnp.bfloat16),
            pltpu.VMEM((local, cuts, columns, width), jnp.bfloat16),
            pltpu.VMEM((local, groups * tok, width), jnp.bfloat16),
            pltpu.VMEM((cuts, groups, tok, columns), jnp.bfloat16),
            pltpu.VMEM((cuts, groups - 1, tok, columns), jnp.bfloat16),
            dma((3 + cuts,)),
            dma((groups - 1,)),
            dma((groups - 1,)),
            dma((groups - 1,)),
            dma((groups - 1,)),
            dma((chunks, 2, reps - 1)),
            dma((chunks, 2, reps - 1)),
            dma((cuts, parts, groups - 1)),
            dma((cuts, parts, groups - 1)),
        ],
        compiler_params=pltpu.CompilerParams(
            collective_id=0, has_side_effects=True, vmem_limit_bytes=56 * 2**20
        ),
        cost_estimate=pl.CostEstimate(
            flops=6 * groups * tok * local * model * width,
            bytes_accessed=6 * local * slab * width + 4 * tok * model,
            transcendentals=groups * tok * local * width,
        ),
    )(tokens, expert_ids.T, route_weights.T, placement_map, w_gate, w_up, down_rows)


def solution(mesh):
    return jax.shard_map(
        on_device,
        mesh=mesh,
        in_specs=(
            P(("rep", "exp"), None),
            P(("rep", "exp"), None),
            P(("rep", "exp"), None),
            P(),
            P("exp", "rep", None),
            P("exp", "rep", None),
            P("exp", "rep", None),
        ),
        out_specs=P(("rep", "exp"), None),
        check_vma=False,
    )
```

```python
import functools

import jax
import jax.numpy as jnp
from jax import lax
from jax.experimental import pallas as pl
from jax.experimental.pallas import tpu as pltpu
from jax.sharding import PartitionSpec as P

LANES = 128
MESH = pl.DeviceIdType.MESH


def flip(index, bit):
    return index + bit - 2 * bit * ((index // bit) % 2)


def flip_all(index, combo):
    bit = 1
    while bit <= combo:
        if combo & bit:
            index = flip(index, bit)
        bit *= 2
    return index


def top_stage(route, combo):
    return max(stage for stage, bit in enumerate(route) if combo & bit)


def kernel(
    reps, groups, cuts,
    tokens, ids, shares, placement, w_gate, w_up, w_down,
    mixed,
    rows_buf, share_buf, gate_up, down, hidden, sums, returned,
    local_sem, token_send, token_recv, share_send, share_recv,
    chunk_send, chunk_recv, back_send, back_recv,
):
    rep, grp = lax.axis_index("rep"), lax.axis_index("exp")
    local, slab, width = w_gate.shape
    tok, model = tokens.shape
    feats = slab // cuts
    total_rows = groups * tok
    chip_bits = [1 << i for i in range(1, reps.bit_length() - 1)]
    routes = [chip_bits + [1], chip_bits[::-1] + [1]]
    stages = len(chip_bits) + 1
    half, piece = slab // 2, feats // 2
    chunks = local + cuts

    masks = [(2 << i) - 1 for i in range(groups.bit_length() - 1)]
    paths = {0: ()}
    for mask in masks:
        paths.update({at ^ mask: path + (mask,) for at, path in list(paths.items())})

    barrier = pltpu.get_barrier_semaphore()
    for bit in routes[0]:
        pl.semaphore_signal(barrier, inc=1, device_id=(flip(rep, bit), grp), device_id_type=MESH)
    for mask in masks:
        pl.semaphore_signal(barrier, inc=1, device_id=(rep, flip_all(grp, mask)), device_id_type=MESH)

    row = lax.broadcasted_iota(jnp.int32, (LANES, tok), 0)
    dense = jnp.zeros((LANES, tok), jnp.float32)
    for k in range(ids.shape[0]):
        dense = dense + jnp.where(row == ids[k : k + 1, :], shares[k : k + 1, :], 0.0)
    lane = lax.broadcasted_iota(jnp.int32, (1, LANES), 1)
    places = jnp.full((1, LANES), -1, jnp.int32)
    for expert in range(placement.shape[0]):
        places = jnp.where(lane == expert, placement[expert], places)
    share_buf[grp] = dense.T

    own_copies = [
        pltpu.make_async_copy(tokens, rows_buf.at[grp], local_sem.at[0]),
        pltpu.make_async_copy(w_gate, gate_up.at[:, 0, pl.ds(rep * slab, slab)], local_sem.at[1]),
        pltpu.make_async_copy(w_up, gate_up.at[:, 1, pl.ds(rep * slab, slab)], local_sem.at[2]),
    ]
    for q in range(cuts):
        own_copies.append(
            pltpu.make_async_copy(
                w_down.at[:, pl.ds(q * feats, feats)],
                down.at[:, q, pl.ds(rep * feats, feats)],
                local_sem.at[3 + q],
            )
        )
    pl.semaphore_wait(barrier, len(routes[0]) + len(masks))

    def token_copies(offset, mask):
        block, slot, to = flip_all(grp, offset), (offset ^ mask) - 1, (rep, flip_all(grp, mask))
        source = tokens if offset == 0 else rows_buf.at[block]
        return (
            pltpu.make_async_remote_copy(
                source, rows_buf.at[block], token_send.at[slot], token_recv.at[slot],
                device_id=to, device_id_type=MESH,
            ),
            pltpu.make_async_remote_copy(
                share_buf.at[block], share_buf.at[block], share_send.at[slot], share_recv.at[slot],
                device_id=to, device_id_type=MESH,
            ),
        )

    def token_arrivals(offset):
        block, slot, to = flip_all(grp, offset), offset - 1, (rep, flip_all(grp, 1))
        return (
            pltpu.make_async_remote_copy(
                rows_buf.at[block], rows_buf.at[block], token_send.at[slot], token_recv.at[slot],
                device_id=to, device_id_type=MESH,
            ),
            pltpu.make_async_remote_copy(
                share_buf.at[block], share_buf.at[block], share_send.at[slot], share_recv.at[slot],
                device_id=to, device_id_type=MESH,
            ),
        )

    def send_tokens(offset, over):
        least = min(paths[offset], default=groups)
        for mask in over:
            if mask < least:
                for copy in token_copies(offset, mask):
                    copy.start()

    def take_tokens(offsets):
        for offset in sorted(offsets, key=lambda at: len(paths[at])):
            for copy in token_arrivals(offset):
                copy.wait_recv()
            send_tokens(offset, masks[::-1])

    def spot(chunk, route, block):
        if chunk < local:
            return gate_up.at[chunk, :, pl.ds(block * slab + route * half, half)]
        return down.at[:, chunk - local, pl.ds(block * feats + route * piece, piece)]

    def parts(chunk, route, block, own):
        if chunk < local:
            at = pl.ds(block * slab + route * half, half)
            if own:
                mine = pl.ds(route * half, half)
                sources = [w_gate.at[chunk, mine], w_up.at[chunk, mine]]
            else:
                sources = [gate_up.at[chunk, 0, at], gate_up.at[chunk, 1, at]]
            return [(sources[0], gate_up.at[chunk, 0, at]), (sources[1], gate_up.at[chunk, 1, at])]
        target = spot(chunk, route, block)
        if own:
            q = chunk - local
            return [(w_down.at[:, pl.ds(q * feats + route * piece, piece)], target)]
        return [(target, target)]

    def pass_on(chunk, route, combo, first_stage):
        block = flip_all(rep, combo)
        for stage in range(first_stage, stages):
            bit = routes[route][stage]
            slot = (combo | bit) - 1
            for source, target in parts(chunk, route, block, combo == 0):
                pltpu.make_async_remote_copy(
                    source, target, chunk_send.at[chunk, route, slot], chunk_recv.at[chunk, route, slot],
                    device_id=(flip(rep, bit), grp), device_id_type=MESH,
                ).start()

    def arrival(chunk, route, combo):
        place = spot(chunk, route, flip_all(rep, combo))
        return pltpu.make_async_remote_copy(
            place, place, chunk_send.at[chunk, route, combo - 1], chunk_recv.at[chunk, route, combo - 1],
            device_id=(flip(rep, 1), grp), device_id_type=MESH,
        )

    def send_own(chunk):
        for route in range(2):
            pass_on(chunk, route, 0, 0)

    def take(chunk, stage):
        for combo in range(1, reps):
            for route in range(2):
                if top_stage(routes[route], combo) == stage:
                    arrival(chunk, route, combo).wait_recv()
                    pass_on(chunk, route, combo, stage + 1)

    block_rows = min(2 * tok, total_rows)
    span = block_rows // tok

    spans = groups // span

    def run_gate_up(member, first, last):
        @pl.loop(first, last)
        def _(i):
            turn = lax.rem(grp // span + i, spans)
            at = pl.ds(turn * span, span)
            x = rows_buf[at].reshape(block_rows, model)
            gate_value = jnp.dot(x, gate_up[member, 0], preferred_element_type=jnp.float32)
            up_value = jnp.dot(x, gate_up[member, 1], preferred_element_type=jnp.float32)
            value = gate_value * up_value / (1.0 + jnp.exp(-gate_value))
            hidden[member, pl.ds(turn * block_rows, block_rows)] = value.astype(jnp.bfloat16)

    columns = reps * feats
    cols = min(256, columns)

    def back_copy(q, part, offset, mask):
        at = pl.ds(part * cols, cols)
        block = flip_all(grp, offset)
        slot = offset - 1
        return pltpu.make_async_remote_copy(
            sums.at[q, block, :, at],
            returned.at[q, slot, :, at],
            back_send.at[q, part, slot],
            back_recv.at[q, part, slot],
            device_id=(rep, flip_all(grp, mask)), device_id_type=MESH,
        )

    def with_first(mask):
        return sorted((at for at in paths if at and paths[at][0] == mask), key=lambda at: -len(paths[at]))

    def run_down(q, part):
        @pl.loop(0, total_rows // block_rows)
        def _(i):
            at = pl.ds(i * span, span)
            dense_rows = share_buf[at].reshape(block_rows, LANES)
            total = jnp.zeros((block_rows, cols), jnp.float32)
            for member in range(local):
                weight = jnp.sum(
                    jnp.where(places == grp * local + member, dense_rows, 0.0), axis=1, keepdims=True
                )
                total = total + weight * lax.dot_general(
                    hidden[member, pl.ds(i * block_rows, block_rows)],
                    down[member, q, part * cols : (part + 1) * cols],
                    (((1,), (1,)), ((), ())),
                    preferred_element_type=jnp.float32,
                )
            sums[q, at, :, part * cols : (part + 1) * cols] = total.astype(jnp.bfloat16).reshape(span, tok, cols)

        send_back(q, part, 0)

    def send_back(q, part, level):
        for offset in with_first(masks[level]):
            back_copy(q, part, offset, masks[level]).start()

    def merge_back(q, part, level):
        for offset in with_first(masks[level]):
            back_copy(q, part, offset, masks[level]).wait_recv()
        for offset in with_first(masks[level]):
            rest = offset ^ masks[level]
            if rest:
                back_copy(q, part, offset, masks[level]).wait_send()
                block = flip_all(grp, rest)
                at = slice(part * cols, (part + 1) * cols)
                sums[q, block, :, at] = (
                    sums[q, block, :, at].astype(jnp.float32) + returned[q, offset - 1, :, at].astype(jnp.float32)
                ).astype(jnp.bfloat16)
        if level + 1 < len(masks):
            send_back(q, part, level + 1)

    send_tokens(0, masks[:0:-1])
    send_own(0)
    for copy in own_copies:
        copy.start()
    send_own(1)
    take(0, 0)
    send_tokens(0, masks[:1])
    far = [offset for offset in range(1, groups) if min(paths[offset]) > 1]
    pieces = [(q, part) for q in range(cuts) for part in range(columns // cols)]
    near_done, all_done, merged, own_sent = 0, 0, 0, 2
    full = min(local - 1, 2)
    for chunk in range(chunks):
        while own_sent < min(chunk + (3 if chunk + 2 < local else 4), chunks):
            send_own(own_sent)
            own_sent += 1
        if chunk + 1 < chunks:
            take(chunk + 1, 0)
        if chunk == full > 0:
            take_tokens([offset for offset in range(2, groups) if offset not in far])
        for stage in range(1, stages):
            if chunk == full and all_done < near_done:
                run_gate_up(all_done, 1, spans)
                all_done += 1
            take(chunk, stage)
        if chunk == 0:
            for copy in own_copies:
                copy.wait()
            take_tokens(far)
            if full == 0:
                take_tokens([offset for offset in range(1, groups) if offset not in far])
        if chunk == 1 == full - 1:
            take_tokens([1])
            while near_done < 2:
                run_gate_up(near_done, 0, 1)
                near_done += 1
        elif chunk == full == 1:
            take_tokens([1])
        if chunk >= full:
            while all_done < min(chunk + 1, local):
                run_gate_up(all_done, 1 if all_done < near_done else 0, spans)
                all_done += 1
        if chunk >= local:
            for part in range(columns // cols):
                run_down(chunk - local, part)
                now = pieces.index((chunk - local, part))
                if now - merged >= 2:
                    merge_back(*pieces[merged], 0)
                    merged += 1
    for offset in range(1, groups):
        for copy in token_arrivals(offset):
            copy.wait_send()
    for chunk in range(chunks):
        for route in range(2):
            for combo in range(1, reps):
                arrival(chunk, route, combo).wait_send()
    while merged < len(pieces):
        merge_back(*pieces[merged], 0)
        merged += 1
    for level in range(1, len(masks) - 1):
        for piece_at in pieces:
            merge_back(*piece_at, level)

    for q, part in pieces:
        merge_back(q, part, len(masks) - 1)
        at = slice(part * cols, (part + 1) * cols)
        value = sums[q, grp, :, at].astype(jnp.float32)
        for mask in masks:
            value = value + returned[q, mask - 1, :, at].astype(jnp.float32)
        value = value.astype(jnp.bfloat16)
        for j in range(cols // feats):
            start = (part * cols // feats + j) * slab + q * feats
            mixed[:, start : start + feats] = value[:, j * feats : (j + 1) * feats]

    for q, part in pieces:
        for level, mask in enumerate(masks):
            for offset in with_first(mask):
                if offset == mask:
                    back_copy(q, part, offset, mask).wait_send()


def on_device(tokens, expert_ids, route_weights, placement_map, w_gate, w_up, down_rows):
    reps, groups = lax.axis_size("rep"), lax.axis_size("exp")
    local, slab, width = w_gate.shape
    tok, model = tokens.shape
    cuts = max(1, slab // 64)
    feats = slab // cuts
    columns = reps * feats
    parts = columns // min(256, columns)
    chunks = local + cuts
    vmem, anywhere = pl.BlockSpec(memory_space=pltpu.VMEM), pl.BlockSpec(memory_space=pl.ANY)
    dma = pltpu.SemaphoreType.DMA
    return pl.pallas_call(
        functools.partial(kernel, reps, groups, cuts),
        out_shape=jax.ShapeDtypeStruct((tok, model), jnp.bfloat16),
        in_specs=[vmem, vmem, vmem, pl.BlockSpec(memory_space=pltpu.SMEM), anywhere, anywhere, anywhere],
        out_specs=vmem,
        scratch_shapes=[
            pltpu.VMEM((groups, tok, model), jnp.bfloat16),
            pltpu.VMEM((groups, tok, LANES), jnp.float32),
            pltpu.VMEM((local, 2, reps * slab, width), jnp.bfloat16),
            pltpu.VMEM((local, cuts, columns, width), jnp.bfloat16),
            pltpu.VMEM((local, groups * tok, width), jnp.bfloat16),
            pltpu.VMEM((cuts, groups, tok, columns), jnp.bfloat16),
            pltpu.VMEM((cuts, groups - 1, tok, columns), jnp.bfloat16),
            dma((3 + cuts,)),
            dma((groups - 1,)),
            dma((groups - 1,)),
            dma((groups - 1,)),
            dma((groups - 1,)),
            dma((chunks, 2, reps - 1)),
            dma((chunks, 2, reps - 1)),
            dma((cuts, parts, groups - 1)),
            dma((cuts, parts, groups - 1)),
        ],
        compiler_params=pltpu.CompilerParams(
            collective_id=0, has_side_effects=True, vmem_limit_bytes=56 * 2**20
        ),
        cost_estimate=pl.CostEstimate(
            flops=6 * groups * tok * local * model * width,
            bytes_accessed=6 * local * slab * width + 4 * tok * model,
            transcendentals=groups * tok * local * width,
        ),
    )(tokens, expert_ids.T, route_weights.T, placement_map, w_gate, w_up, down_rows)


def solution(mesh):
    return jax.shard_map(
        on_device,
        mesh=mesh,
        in_specs=(
            P(("rep", "exp"), None),
            P(("rep", "exp"), None),
            P(("rep", "exp"), None),
            P(),
            P("exp", "rep", None),
            P("exp", "rep", None),
            P("exp", "rep", None),
        ),
        out_specs=P(("rep", "exp"), None),
        check_vma=False,
    )
```

```python
import functools

import jax
import jax.numpy as jnp
from jax import lax
from jax.experimental import pallas as pl
from jax.experimental.pallas import tpu as pltpu
from jax.sharding import PartitionSpec as P

LANES = 128
MESH = pl.DeviceIdType.MESH


def flip(index, bit):
    return index + bit - 2 * bit * ((index // bit) % 2)


def flip_all(index, combo):
    bit = 1
    while bit <= combo:
        if combo & bit:
            index = flip(index, bit)
        bit *= 2
    return index


def top_stage(route, combo):
    return max(stage for stage, bit in enumerate(route) if combo & bit)


def kernel(
    reps, groups, cuts,
    tokens, ids, shares, placement, w_gate, w_up, w_down,
    mixed,
    rows_buf, share_buf, weights, gate_up, down, hidden, sums, returned,
    local_sem, token_send, token_recv, share_send, share_recv,
    chunk_send, chunk_recv, back_send, back_recv,
):
    rep, grp = lax.axis_index("rep"), lax.axis_index("exp")
    local, slab, width = w_gate.shape
    tok, model = tokens.shape
    feats = slab // cuts
    total_rows = groups * tok
    chip_bits = [1 << i for i in range(1, reps.bit_length() - 1)]
    routes = [chip_bits + [1], chip_bits[::-1] + [1]]
    stages = len(chip_bits) + 1
    half, piece = slab // 2, feats // 2
    chunks = local + cuts

    masks = [(2 << i) - 1 for i in range(groups.bit_length() - 1)]
    paths = {0: ()}
    for mask in masks:
        paths.update({at ^ mask: path + (mask,) for at, path in list(paths.items())})

    barrier = pltpu.get_barrier_semaphore()
    for bit in routes[0]:
        pl.semaphore_signal(barrier, inc=1, device_id=(flip(rep, bit), grp), device_id_type=MESH)
    for mask in masks:
        pl.semaphore_signal(barrier, inc=1, device_id=(rep, flip_all(grp, mask)), device_id_type=MESH)

    row = lax.broadcasted_iota(jnp.int32, (LANES, tok), 0)
    dense = jnp.zeros((LANES, tok), jnp.float32)
    for k in range(ids.shape[0]):
        dense = dense + jnp.where(row == ids[k : k + 1, :], shares[k : k + 1, :], 0.0)
    lane = lax.broadcasted_iota(jnp.int32, (1, LANES), 1)
    places = jnp.full((1, LANES), -1, jnp.int32)
    for expert in range(placement.shape[0]):
        places = jnp.where(lane == expert, placement[expert], places)
    share_buf[grp] = dense.T

    own_copies = [
        pltpu.make_async_copy(tokens, rows_buf.at[grp], local_sem.at[0]),
        pltpu.make_async_copy(w_gate, gate_up.at[:, 0, pl.ds(rep * slab, slab)], local_sem.at[1]),
        pltpu.make_async_copy(w_up, gate_up.at[:, 1, pl.ds(rep * slab, slab)], local_sem.at[2]),
    ]
    for q in range(cuts):
        own_copies.append(
            pltpu.make_async_copy(
                w_down.at[:, pl.ds(q * feats, feats)],
                down.at[:, q, pl.ds(rep * feats, feats)],
                local_sem.at[3 + q],
            )
        )
    pl.semaphore_wait(barrier, len(routes[0]) + len(masks))

    def token_copies(offset, mask):
        block, slot, to = flip_all(grp, offset), (offset ^ mask) - 1, (rep, flip_all(grp, mask))
        source = tokens if offset == 0 else rows_buf.at[block]
        return (
            pltpu.make_async_remote_copy(
                source, rows_buf.at[block], token_send.at[slot], token_recv.at[slot],
                device_id=to, device_id_type=MESH,
            ),
            pltpu.make_async_remote_copy(
                share_buf.at[block], share_buf.at[block], share_send.at[slot], share_recv.at[slot],
                device_id=to, device_id_type=MESH,
            ),
        )

    def token_arrivals(offset):
        block, slot, to = flip_all(grp, offset), offset - 1, (rep, flip_all(grp, 1))
        return (
            pltpu.make_async_remote_copy(
                rows_buf.at[block], rows_buf.at[block], token_send.at[slot], token_recv.at[slot],
                device_id=to, device_id_type=MESH,
            ),
            pltpu.make_async_remote_copy(
                share_buf.at[block], share_buf.at[block], share_send.at[slot], share_recv.at[slot],
                device_id=to, device_id_type=MESH,
            ),
        )

    def send_tokens(offset, over):
        least = min(paths[offset], default=groups)
        for mask in over:
            if mask < least:
                for copy in token_copies(offset, mask):
                    copy.start()

    def take_tokens(offsets):
        for offset in sorted(offsets, key=lambda at: len(paths[at])):
            for copy in token_arrivals(offset):
                copy.wait_recv()
            send_tokens(offset, masks[::-1])

    def spot(chunk, route, block):
        if chunk < local:
            return gate_up.at[chunk, :, pl.ds(block * slab + route * half, half)]
        return down.at[:, chunk - local, pl.ds(block * feats + route * piece, piece)]

    def parts(chunk, route, block, own):
        if chunk < local:
            at = pl.ds(block * slab + route * half, half)
            if own:
                mine = pl.ds(route * half, half)
                sources = [w_gate.at[chunk, mine], w_up.at[chunk, mine]]
            else:
                sources = [gate_up.at[chunk, 0, at], gate_up.at[chunk, 1, at]]
            return [(sources[0], gate_up.at[chunk, 0, at]), (sources[1], gate_up.at[chunk, 1, at])]
        target = spot(chunk, route, block)
        if own:
            q = chunk - local
            return [(w_down.at[:, pl.ds(q * feats + route * piece, piece)], target)]
        return [(target, target)]

    def pass_on(chunk, route, combo, first_stage):
        block = flip_all(rep, combo)
        for stage in range(first_stage, stages):
            bit = routes[route][stage]
            slot = (combo | bit) - 1
            for source, target in parts(chunk, route, block, combo == 0):
                pltpu.make_async_remote_copy(
                    source, target, chunk_send.at[chunk, route, slot], chunk_recv.at[chunk, route, slot],
                    device_id=(flip(rep, bit), grp), device_id_type=MESH,
                ).start()

    def arrival(chunk, route, combo):
        place = spot(chunk, route, flip_all(rep, combo))
        return pltpu.make_async_remote_copy(
            place, place, chunk_send.at[chunk, route, combo - 1], chunk_recv.at[chunk, route, combo - 1],
            device_id=(flip(rep, 1), grp), device_id_type=MESH,
        )

    def send_own(chunk):
        for route in range(2):
            pass_on(chunk, route, 0, 0)

    def take(chunk, stage):
        for combo in range(1, reps):
            for route in range(2):
                if top_stage(routes[route], combo) == stage:
                    arrival(chunk, route, combo).wait_recv()
                    pass_on(chunk, route, combo, stage + 1)

    block_rows = min(2 * tok, total_rows)
    span = block_rows // tok

    spans = groups // span

    def run_gate_up(member, first, last):
        @pl.loop(first, last)
        def _(i):
            turn = lax.rem(grp // span + i, spans)
            at = pl.ds(turn * span, span)
            x = rows_buf[at].reshape(block_rows, model)
            gate_value = jnp.dot(x, gate_up[member, 0], preferred_element_type=jnp.float32)
            up_value = jnp.dot(x, gate_up[member, 1], preferred_element_type=jnp.float32)
            value = gate_value * up_value / (1.0 + jnp.exp(-gate_value))
            hidden[member, pl.ds(turn * block_rows, block_rows)] = value.astype(jnp.bfloat16)

    columns = reps * feats
    cols = min(256, columns)

    def back_copy(q, part, offset, mask):
        at = pl.ds(part * cols, cols)
        block = flip_all(grp, offset)
        slot = offset - 1
        return pltpu.make_async_remote_copy(
            sums.at[q, block, :, at],
            returned.at[q, slot, :, at],
            back_send.at[q, part, slot],
            back_recv.at[q, part, slot],
            device_id=(rep, flip_all(grp, mask)), device_id_type=MESH,
        )

    def with_first(mask):
        return sorted((at for at in paths if at and paths[at][0] == mask), key=lambda at: -len(paths[at]))

    wide_rows = min(4 * tok, total_rows)
    wide = wide_rows // tok

    def spread_weights():
        for member in range(local):

            @pl.loop(0, groups)
            def _(block):
                kept = jnp.where(places == grp * local + member, share_buf[block], 0.0)
                weights[member, block] = jnp.broadcast_to(jnp.sum(kept, axis=1, keepdims=True), (tok, LANES))

    def run_down(q, part):
        @pl.loop(0, total_rows // wide_rows)
        def _(i):
            at = pl.ds(i * wide, wide)
            total = jnp.zeros((wide_rows, cols), jnp.float32)
            for member in range(local):
                weight = weights[member, at].reshape(wide_rows, LANES)
                total = total + jnp.concatenate([weight] * (cols // LANES), axis=1) * lax.dot_general(
                    hidden[member, pl.ds(i * wide_rows, wide_rows)],
                    down[member, q, part * cols : (part + 1) * cols],
                    (((1,), (1,)), ((), ())),
                    preferred_element_type=jnp.float32,
                )
            sums[q, at, :, part * cols : (part + 1) * cols] = total.astype(jnp.bfloat16).reshape(wide, tok, cols)

    def send_back(q, part, level, ends=(False, True)):
        for offset in with_first(masks[level]):
            if (len(paths[offset]) == 1) not in ends:
                continue
            back_copy(q, part, offset, masks[level]).start()

    def merge_back(q, part, level):
        for offset in with_first(masks[level]):
            back_copy(q, part, offset, masks[level]).wait_recv()
        for offset in with_first(masks[level]):
            rest = offset ^ masks[level]
            if rest:
                back_copy(q, part, offset, masks[level]).wait_send()
                block = flip_all(grp, rest)
                at = slice(part * cols, (part + 1) * cols)
                sums[q, block, :, at] = (
                    sums[q, block, :, at].astype(jnp.float32) + returned[q, offset - 1, :, at].astype(jnp.float32)
                ).astype(jnp.bfloat16)
        if level + 1 < len(masks):
            send_back(q, part, level + 1)

    send_tokens(0, masks[:0:-1])
    send_own(0)
    for copy in own_copies:
        copy.start()
    send_own(1)
    take(0, 0)
    send_tokens(0, masks[:1])
    far = [offset for offset in range(1, groups) if min(paths[offset]) > 1]
    pieces = [(q, part) for q in range(cuts) for part in range(columns // cols)]
    near_done, all_done, merged, own_sent = 0, 0, 0, 2
    full = min(local - 1, 2)
    for chunk in range(chunks):
        while own_sent < min(chunk + (3 if chunk + 2 < local else 4), chunks):
            send_own(own_sent)
            own_sent += 1
        if chunk + 1 < chunks:
            take(chunk + 1, 0)
        if chunk == full > 0:
            take_tokens([offset for offset in range(2, groups) if offset not in far])
        for stage in range(1, stages):
            if chunk == full and all_done < near_done:
                run_gate_up(all_done, 1, spans)
                all_done += 1
            take(chunk, stage)
        if chunk == 0:
            for copy in own_copies:
                copy.wait()
            take_tokens(far)
            if full == 0:
                take_tokens([offset for offset in range(1, groups) if offset not in far])
        if chunk == 1 == full - 1:
            take_tokens([1])
            while near_done < 2:
                run_gate_up(near_done, 0, 1)
                near_done += 1
        elif chunk == full == 1:
            take_tokens([1])
        if chunk >= full:
            while all_done < min(chunk + 1, local):
                run_gate_up(all_done, 1 if all_done < near_done else 0, spans)
                all_done += 1
        if chunk == min(full, local - 1):
            spread_weights()
        if chunk >= local:
            for part in range(columns // cols):
                run_down(chunk - local, part)
                send_back(chunk - local, part, 0, (False,) if chunk == chunks - 1 else (False, True))
                now = pieces.index((chunk - local, part))
                if now - merged >= 2 and pieces[merged][0] < cuts - 1:
                    merge_back(*pieces[merged], 0)
                    merged += 1
    for part in range(columns // cols):
        send_back(cuts - 1, part, 0, (True,))
    while merged < len(pieces):
        merge_back(*pieces[merged], 0)
        merged += 1
    for level in range(1, len(masks) - 1):
        for piece_at in pieces:
            merge_back(*piece_at, level)

    for offset in range(1, groups):
        for copy in token_arrivals(offset):
            copy.wait_send()
    for chunk in range(chunks):
        for route in range(2):
            for combo in range(1, reps):
                arrival(chunk, route, combo).wait_send()

    for q, part in pieces:
        merge_back(q, part, len(masks) - 1)
        at = slice(part * cols, (part + 1) * cols)
        value = sums[q, grp, :, at].astype(jnp.float32)
        for mask in masks:
            value = value + returned[q, mask - 1, :, at].astype(jnp.float32)
        value = value.astype(jnp.bfloat16)
        for j in range(cols // feats):
            start = (part * cols // feats + j) * slab + q * feats
            mixed[:, start : start + feats] = value[:, j * feats : (j + 1) * feats]

    for q, part in pieces:
        for level, mask in enumerate(masks):
            for offset in with_first(mask):
                if offset == mask:
                    back_copy(q, part, offset, mask).wait_send()


def on_device(tokens, expert_ids, route_weights, placement_map, w_gate, w_up, down_rows):
    reps, groups = lax.axis_size("rep"), lax.axis_size("exp")
    local, slab, width = w_gate.shape
    tok, model = tokens.shape
    cuts = max(1, slab // 64)
    feats = slab // cuts
    columns = reps * feats
    parts = columns // min(256, columns)
    chunks = local + cuts
    vmem, anywhere = pl.BlockSpec(memory_space=pltpu.VMEM), pl.BlockSpec(memory_space=pl.ANY)
    dma = pltpu.SemaphoreType.DMA
    return pl.pallas_call(
        functools.partial(kernel, reps, groups, cuts),
        out_shape=jax.ShapeDtypeStruct((tok, model), jnp.bfloat16),
        in_specs=[vmem, vmem, vmem, pl.BlockSpec(memory_space=pltpu.SMEM), anywhere, anywhere, anywhere],
        out_specs=vmem,
        scratch_shapes=[
            pltpu.VMEM((groups, tok, model), jnp.bfloat16),
            pltpu.VMEM((groups, tok, LANES), jnp.float32),
            pltpu.VMEM((local, groups, tok, LANES), jnp.float32),
            pltpu.VMEM((local, 2, reps * slab, width), jnp.bfloat16),
            pltpu.VMEM((local, cuts, columns, width), jnp.bfloat16),
            pltpu.VMEM((local, groups * tok, width), jnp.bfloat16),
            pltpu.VMEM((cuts, groups, tok, columns), jnp.bfloat16),
            pltpu.VMEM((cuts, groups - 1, tok, columns), jnp.bfloat16),
            dma((3 + cuts,)),
            dma((groups - 1,)),
            dma((groups - 1,)),
            dma((groups - 1,)),
            dma((groups - 1,)),
            dma((chunks, 2, reps - 1)),
            dma((chunks, 2, reps - 1)),
            dma((cuts, parts, groups - 1)),
            dma((cuts, parts, groups - 1)),
        ],
        compiler_params=pltpu.CompilerParams(
            collective_id=0, has_side_effects=True, vmem_limit_bytes=56 * 2**20
        ),
        cost_estimate=pl.CostEstimate(
            flops=6 * groups * tok * local * model * width,
            bytes_accessed=6 * local * slab * width + 4 * tok * model,
            transcendentals=groups * tok * local * width,
        ),
    )(tokens, expert_ids.T, route_weights.T, placement_map, w_gate, w_up, down_rows)


def solution(mesh):
    return jax.shard_map(
        on_device,
        mesh=mesh,
        in_specs=(
            P(("rep", "exp"), None),
            P(("rep", "exp"), None),
            P(("rep", "exp"), None),
            P(),
            P("exp", "rep", None),
            P("exp", "rep", None),
            P("exp", "rep", None),
        ),
        out_specs=P(("rep", "exp"), None),
        check_vma=False,
    )
```

```python
import functools

import jax
import jax.numpy as jnp
from jax import lax
from jax.experimental import pallas as pl
from jax.experimental.pallas import tpu as pltpu
from jax.sharding import PartitionSpec as P

LANES = 128
MESH = pl.DeviceIdType.MESH


def flip(index, bit):
    return index + bit - 2 * bit * ((index // bit) % 2)


def flip_all(index, combo):
    bit = 1
    while bit <= combo:
        if combo & bit:
            index = flip(index, bit)
        bit *= 2
    return index


def top_stage(route, combo):
    return max(stage for stage, bit in enumerate(route) if combo & bit)


def kernel(
    reps, groups, cuts,
    tokens, ids, shares, placement, w_gate, w_up, w_down,
    mixed,
    rows_buf, share_buf, weights, gate_up, down, hidden, sums, returned,
    local_sem, token_send, token_recv, share_send, share_recv,
    chunk_send, chunk_recv, back_send, back_recv,
):
    rep, grp = lax.axis_index("rep"), lax.axis_index("exp")
    local, slab, width = w_gate.shape
    tok, model = tokens.shape
    feats = slab // cuts
    total_rows = groups * tok
    chip_bits = [1 << i for i in range(1, reps.bit_length() - 1)]
    routes = [chip_bits + [1], chip_bits[::-1] + [1]]
    stages = len(chip_bits) + 1
    half, piece = slab // 2, feats // 2
    chunks = local + cuts

    masks = [(2 << i) - 1 for i in range(groups.bit_length() - 1)]
    paths = {0: ()}
    for mask in masks:
        paths.update({at ^ mask: path + (mask,) for at, path in list(paths.items())})

    barrier = pltpu.get_barrier_semaphore()
    for bit in routes[0]:
        pl.semaphore_signal(barrier, inc=1, device_id=(flip(rep, bit), grp), device_id_type=MESH)
    for mask in masks:
        pl.semaphore_signal(barrier, inc=1, device_id=(rep, flip_all(grp, mask)), device_id_type=MESH)

    row = lax.broadcasted_iota(jnp.int32, (LANES, tok), 0)
    dense = jnp.zeros((LANES, tok), jnp.float32)
    for k in range(ids.shape[0]):
        dense = dense + jnp.where(row == ids[k : k + 1, :], shares[k : k + 1, :], 0.0)
    lane = lax.broadcasted_iota(jnp.int32, (1, LANES), 1)
    places = jnp.full((1, LANES), -1, jnp.int32)
    for expert in range(placement.shape[0]):
        places = jnp.where(lane == expert, placement[expert], places)
    share_buf[grp] = dense.T

    own_copies = [
        pltpu.make_async_copy(tokens, rows_buf.at[grp], local_sem.at[0]),
        pltpu.make_async_copy(w_gate, gate_up.at[:, 0, pl.ds(rep * slab, slab)], local_sem.at[1]),
        pltpu.make_async_copy(w_up, gate_up.at[:, 1, pl.ds(rep * slab, slab)], local_sem.at[2]),
    ]
    for q in range(cuts):
        own_copies.append(
            pltpu.make_async_copy(
                w_down.at[:, pl.ds(q * feats, feats)],
                down.at[:, q, pl.ds(rep * feats, feats)],
                local_sem.at[3 + q],
            )
        )
    pl.semaphore_wait(barrier, len(routes[0]) + len(masks))

    def token_copies(offset, mask):
        block, slot, to = flip_all(grp, offset), (offset ^ mask) - 1, (rep, flip_all(grp, mask))
        source = tokens if offset == 0 else rows_buf.at[block]
        return (
            pltpu.make_async_remote_copy(
                source, rows_buf.at[block], token_send.at[slot], token_recv.at[slot],
                device_id=to, device_id_type=MESH,
            ),
            pltpu.make_async_remote_copy(
                share_buf.at[block], share_buf.at[block], share_send.at[slot], share_recv.at[slot],
                device_id=to, device_id_type=MESH,
            ),
        )

    def token_arrivals(offset):
        block, slot, to = flip_all(grp, offset), offset - 1, (rep, flip_all(grp, 1))
        return (
            pltpu.make_async_remote_copy(
                rows_buf.at[block], rows_buf.at[block], token_send.at[slot], token_recv.at[slot],
                device_id=to, device_id_type=MESH,
            ),
            pltpu.make_async_remote_copy(
                share_buf.at[block], share_buf.at[block], share_send.at[slot], share_recv.at[slot],
                device_id=to, device_id_type=MESH,
            ),
        )

    def send_tokens(offset, over):
        least = min(paths[offset], default=groups)
        for mask in over:
            if mask < least:
                for copy in token_copies(offset, mask):
                    copy.start()

    def take_tokens(offsets):
        for offset in sorted(offsets, key=lambda at: len(paths[at])):
            for copy in token_arrivals(offset):
                copy.wait_recv()
            send_tokens(offset, masks[::-1])

    def spot(chunk, route, block):
        if chunk < local:
            return gate_up.at[chunk, :, pl.ds(block * slab + route * half, half)]
        return down.at[:, chunk - local, pl.ds(block * feats + route * piece, piece)]

    def parts(chunk, route, block, own):
        if chunk < local:
            at = pl.ds(block * slab + route * half, half)
            if own:
                mine = pl.ds(route * half, half)
                sources = [w_gate.at[chunk, mine], w_up.at[chunk, mine]]
            else:
                sources = [gate_up.at[chunk, 0, at], gate_up.at[chunk, 1, at]]
            return [(sources[0], gate_up.at[chunk, 0, at]), (sources[1], gate_up.at[chunk, 1, at])]
        target = spot(chunk, route, block)
        if own:
            q = chunk - local
            return [(w_down.at[:, pl.ds(q * feats + route * piece, piece)], target)]
        return [(target, target)]

    def pass_on(chunk, route, combo, first_stage):
        block = flip_all(rep, combo)
        for stage in range(first_stage, stages):
            bit = routes[route][stage]
            slot = (combo | bit) - 1
            for source, target in parts(chunk, route, block, combo == 0):
                pltpu.make_async_remote_copy(
                    source, target, chunk_send.at[chunk, route, slot], chunk_recv.at[chunk, route, slot],
                    device_id=(flip(rep, bit), grp), device_id_type=MESH,
                ).start()

    def arrival(chunk, route, combo):
        place = spot(chunk, route, flip_all(rep, combo))
        return pltpu.make_async_remote_copy(
            place, place, chunk_send.at[chunk, route, combo - 1], chunk_recv.at[chunk, route, combo - 1],
            device_id=(flip(rep, 1), grp), device_id_type=MESH,
        )

    def send_own(chunk):
        for route in range(2):
            pass_on(chunk, route, 0, 0)

    def take(chunk, stage):
        for combo in range(1, reps):
            for route in range(2):
                if top_stage(routes[route], combo) == stage:
                    arrival(chunk, route, combo).wait_recv()
                    pass_on(chunk, route, combo, stage + 1)

    block_rows = min(2 * tok, total_rows)
    span = block_rows // tok

    spans = groups // span

    def run_gate_up(member, first, last):
        @pl.loop(first, last)
        def _(i):
            turn = lax.rem(grp // span + i, spans)
            at = pl.ds(turn * span, span)
            x = rows_buf[at].reshape(block_rows, model)
            gate_value = jnp.dot(x, gate_up[member, 0], preferred_element_type=jnp.float32)
            up_value = jnp.dot(x, gate_up[member, 1], preferred_element_type=jnp.float32)
            value = gate_value * up_value / (1.0 + jnp.exp(-gate_value))
            hidden[member, pl.ds(turn * block_rows, block_rows)] = value.astype(jnp.bfloat16)

    columns = reps * feats
    cols = min(256, columns)

    def back_copy(q, part, offset, mask):
        at = pl.ds(part * cols, cols)
        block = flip_all(grp, offset)
        slot = offset - 1
        return pltpu.make_async_remote_copy(
            sums.at[q, block, :, at],
            returned.at[q, slot, :, at],
            back_send.at[q, part, slot],
            back_recv.at[q, part, slot],
            device_id=(rep, flip_all(grp, mask)), device_id_type=MESH,
        )

    def with_first(mask):
        return sorted((at for at in paths if at and paths[at][0] == mask), key=lambda at: -len(paths[at]))

    wide_rows = min(4 * tok, total_rows)
    wide = wide_rows // tok

    def spread_weights():
        for member in range(local):

            @pl.loop(0, groups)
            def _(block):
                kept = jnp.where(places == grp * local + member, share_buf[block], 0.0)
                weights[member, block] = jnp.broadcast_to(jnp.sum(kept, axis=1, keepdims=True), (tok, LANES))

    def run_down(q, part):
        @pl.loop(0, total_rows // wide_rows)
        def _(i):
            at = pl.ds(i * wide, wide)
            total = jnp.zeros((wide_rows, cols), jnp.float32)
            for member in range(local):
                weight = weights[member, at].reshape(wide_rows, LANES)
                total = total + jnp.concatenate([weight] * (cols // LANES), axis=1) * lax.dot_general(
                    hidden[member, pl.ds(i * wide_rows, wide_rows)],
                    down[member, q, part * cols : (part + 1) * cols],
                    (((1,), (1,)), ((), ())),
                    preferred_element_type=jnp.float32,
                )
            sums[q, at, :, part * cols : (part + 1) * cols] = total.astype(jnp.bfloat16).reshape(wide, tok, cols)

    def send_back(q, part, level, ends=(False, True)):
        for offset in with_first(masks[level]):
            if (len(paths[offset]) == 1) not in ends:
                continue
            back_copy(q, part, offset, masks[level]).start()

    def merge_back(q, part, level):
        for offset in with_first(masks[level]):
            back_copy(q, part, offset, masks[level]).wait_recv()
        for offset in with_first(masks[level]):
            rest = offset ^ masks[level]
            if rest:
                back_copy(q, part, offset, masks[level]).wait_send()
                block = flip_all(grp, rest)
                at = slice(part * cols, (part + 1) * cols)
                sums[q, block, :, at] = (
                    sums[q, block, :, at].astype(jnp.float32) + returned[q, offset - 1, :, at].astype(jnp.float32)
                ).astype(jnp.bfloat16)
        if level + 1 < len(masks):
            send_back(q, part, level + 1)

    send_tokens(0, masks[:0:-1])
    send_own(0)
    for copy in own_copies:
        copy.start()
    send_own(1)
    take(0, 0)
    send_tokens(0, masks[:1])
    far = [offset for offset in range(1, groups) if min(paths[offset]) > 1]
    pieces = [(q, part) for q in range(cuts) for part in range(columns // cols)]
    near_done, all_done, merged, own_sent = 0, 0, 0, 2
    full = min(local - 1, 2)
    for chunk in range(chunks):
        while own_sent < min(chunk + (3 if chunk < local else 4), chunks):
            send_own(own_sent)
            own_sent += 1
        if chunk + 1 < chunks:
            take(chunk + 1, 0)
        if chunk == full > 0:
            take_tokens([offset for offset in range(2, groups) if offset not in far])
        for stage in range(1, stages):
            if chunk == full and all_done < near_done:
                run_gate_up(all_done, 1, spans)
                all_done += 1
            take(chunk, stage)
        if chunk == 0:
            for copy in own_copies:
                copy.wait()
            take_tokens(far)
            if full == 0:
                take_tokens([offset for offset in range(1, groups) if offset not in far])
        if chunk == 1 == full - 1:
            take_tokens([1])
            while near_done < 2:
                run_gate_up(near_done, 0, 1)
                near_done += 1
        elif chunk == full == 1:
            take_tokens([1])
        if chunk >= full:
            while all_done < min(chunk + 1, local):
                run_gate_up(all_done, 1 if all_done < near_done else 0, spans)
                all_done += 1
        if chunk == min(full, local - 1):
            spread_weights()
        if chunk >= local:
            for part in range(columns // cols):
                run_down(chunk - local, part)
                send_back(chunk - local, part, 0, (False,) if chunk == chunks - 1 else (False, True))
                now = pieces.index((chunk - local, part))
                if now - merged >= 2 and pieces[merged][0] < cuts - 1:
                    merge_back(*pieces[merged], 0)
                    merged += 1
    for part in range(columns // cols):
        send_back(cuts - 1, part, 0, (True,))
    while merged < len(pieces):
        merge_back(*pieces[merged], 0)
        merged += 1
    for level in range(1, len(masks) - 1):
        for piece_at in pieces:
            merge_back(*piece_at, level)

    for offset in range(1, groups):
        for copy in token_arrivals(offset):
            copy.wait_send()
    for chunk in range(chunks):
        for route in range(2):
            for combo in range(1, reps):
                arrival(chunk, route, combo).wait_send()

    for q, part in pieces:
        merge_back(q, part, len(masks) - 1)
        at = slice(part * cols, (part + 1) * cols)
        value = sums[q, grp, :, at].astype(jnp.float32)
        for mask in masks:
            value = value + returned[q, mask - 1, :, at].astype(jnp.float32)
        value = value.astype(jnp.bfloat16)
        for j in range(cols // feats):
            start = (part * cols // feats + j) * slab + q * feats
            mixed[:, start : start + feats] = value[:, j * feats : (j + 1) * feats]

    for q, part in pieces:
        for level, mask in enumerate(masks):
            for offset in with_first(mask):
                if offset == mask:
                    back_copy(q, part, offset, mask).wait_send()


def on_device(tokens, expert_ids, route_weights, placement_map, w_gate, w_up, down_rows):
    reps, groups = lax.axis_size("rep"), lax.axis_size("exp")
    local, slab, width = w_gate.shape
    tok, model = tokens.shape
    cuts = max(1, slab // 64)
    feats = slab // cuts
    columns = reps * feats
    parts = columns // min(256, columns)
    chunks = local + cuts
    vmem, anywhere = pl.BlockSpec(memory_space=pltpu.VMEM), pl.BlockSpec(memory_space=pl.ANY)
    dma = pltpu.SemaphoreType.DMA
    return pl.pallas_call(
        functools.partial(kernel, reps, groups, cuts),
        out_shape=jax.ShapeDtypeStruct((tok, model), jnp.bfloat16),
        in_specs=[vmem, vmem, vmem, pl.BlockSpec(memory_space=pltpu.SMEM), anywhere, anywhere, anywhere],
        out_specs=vmem,
        scratch_shapes=[
            pltpu.VMEM((groups, tok, model), jnp.bfloat16),
            pltpu.VMEM((groups, tok, LANES), jnp.float32),
            pltpu.VMEM((local, groups, tok, LANES), jnp.float32),
            pltpu.VMEM((local, 2, reps * slab, width), jnp.bfloat16),
            pltpu.VMEM((local, cuts, columns, width), jnp.bfloat16),
            pltpu.VMEM((local, groups * tok, width), jnp.bfloat16),
            pltpu.VMEM((cuts, groups, tok, columns), jnp.bfloat16),
            pltpu.VMEM((cuts, groups - 1, tok, columns), jnp.bfloat16),
            dma((3 + cuts,)),
            dma((groups - 1,)),
            dma((groups - 1,)),
            dma((groups - 1,)),
            dma((groups - 1,)),
            dma((chunks, 2, reps - 1)),
            dma((chunks, 2, reps - 1)),
            dma((cuts, parts, groups - 1)),
            dma((cuts, parts, groups - 1)),
        ],
        compiler_params=pltpu.CompilerParams(
            collective_id=0, has_side_effects=True, vmem_limit_bytes=56 * 2**20
        ),
        cost_estimate=pl.CostEstimate(
            flops=6 * groups * tok * local * model * width,
            bytes_accessed=6 * local * slab * width + 4 * tok * model,
            transcendentals=groups * tok * local * width,
        ),
    )(tokens, expert_ids.T, route_weights.T, placement_map, w_gate, w_up, down_rows)


def solution(mesh):
    return jax.shard_map(
        on_device,
        mesh=mesh,
        in_specs=(
            P(("rep", "exp"), None),
            P(("rep", "exp"), None),
            P(("rep", "exp"), None),
            P(),
            P("exp", "rep", None),
            P("exp", "rep", None),
            P("exp", "rep", None),
        ),
        out_specs=P(("rep", "exp"), None),
        check_vma=False,
    )
```
